512 devices in a mesh: fsdp: 16 (over z_hi, y), dp: 32 (over x, z_lo, core).
Axes of the slice: x: 4, y: 4, z: 16 (z_hi: 4, z_lo: 4; z = z_hi * 4 + z_lo), core: 2. Of those that a mesh axis runs over, the one named last changes fastest.
Arguments:
- noise_embed: bfloat16 [8192, 1024], P(('fsdp', 'dp')), may hold values from -6 to 6
- action_embed: bfloat16 [8192, 1024], P(('fsdp', 'dp')), may hold values from -6 to 6
- prefix_kv: bfloat16 [2, 512, 256, 256], P(None, ('fsdp', 'dp')), may hold values from -6 to 6
- flow_step: int32 [512], P(('fsdp', 'dp')), may hold values from 0 to 9
- action_mask: int32 [8192], P(('fsdp', 'dp')), may hold values 0 or 1
- w_up: bfloat16 [1024, 4096], P(None, 'fsdp'), may hold values from -0.1875 to 0.1875
- w_down: bfloat16 [4096, 1024], P('fsdp'), may hold values from -0.09375 to 0.09375
- query_grad: float32 [1024, 4096], P(None, 'fsdp'), may hold values from -6 to 6
Outputs:
- inverse_hvp: float32 [1024, 4096], P(None, 'fsdp')
- scores: float32 [512], P(('fsdp', 'dp'))
The draws below stay inside these ranges and needn't reach their ends.
All inputs are finite; a program needn't handle non-finite values. No bound on the sum of `action_mask` on one device may be relied on, other than what follows from the above.
Results may differ from the reference program's by a relative error of at most 0.03.
Values may be sent and summed in bfloat16 or wider, within the bound.
No kernel may reach another device: no remote copies, remote signals or barrier semaphores. Data moves between devices by JAX's collectives and lax.ppermute only.
A program may use at most 64 MiB of HBM per device.

```python
import math
import jax
import jax.numpy as jnp
from jax import lax

D = 1024
FF = 4096
CHANNEL_SPAN = 256
HEADS = 4
PREFIX = 256
ACT = 16
STEPS_T = 10
ITERS = 2
DEMOS = 512
TOKENS = 8192


def place_ends(array, stream_key, smallest, top_value):
    dims = array.shape
    spot = [jax.random.randint(jax.random.fold_in(stream_key, axis), (), 0, dims[axis]) for axis in range(len(dims))]
    array = array.at[tuple(spot)].set(smallest)
    longest = dims.index(max(dims))
    spot[longest] = (spot[longest] + 1) % dims[longest]
    return array.at[tuple(spot)].set(top_value)


def steps_of(key, dims, pieces, smallest, top_value):
    def one(dim, parts):
        draws = jax.random.uniform(jax.random.fold_in(jax.random.fold_in(key, 6), dim), (parts,), jnp.float32, smallest / len(pieces), top_value / len(pieces))
        return jnp.repeat(jnp.exp(draws), dims[dim] // parts).reshape((-1,) + (1,) * (len(dims) - dim - 1))

    loudness = one(*pieces[0])
    for cut in pieces[1:]:
        loudness = loudness * one(*cut)
    return loudness


def bell_draw(key, extent, width, most, shards=(), dtype=jnp.bfloat16):
    values = width * jax.random.normal(key, extent, jnp.float32)
    if shards:
        values = values * steps_of(key, extent, shards, -0.22, 0.18)
    return jnp.clip(values, -most, most).astype(dtype)


def setup_inputs(seed: int = 0) -> dict:
    streams_of = jax.random.split(jax.random.key(seed), 9)
    noise_embed = bell_draw(streams_of[0], (TOKENS, D), 1.0, 6.0, ((0, 512),))
    action_embed = bell_draw(streams_of[1], (TOKENS, D), 1.0, 6.0, ((0, 512),))
    prefix_kv = bell_draw(streams_of[2], (2, DEMOS, PREFIX, CHANNEL_SPAN), 1.0, 6.0, ((1, 512),))
    flow_step = place_ends(jax.random.randint(streams_of[3], (DEMOS,), 0, STEPS_T), jax.random.fold_in(streams_of[3], 1), 0, STEPS_T - 1).astype(jnp.int32)
    action_mask = place_ends((jax.random.randint(streams_of[4], (TOKENS,), 0, 4) < 3).astype(jnp.int32), jax.random.fold_in(streams_of[4], 1), 0, 1)
    w_up = bell_draw(streams_of[5], (D, FF), D ** -0.5, 0.1875, ((1, 16),))
    w_down = bell_draw(streams_of[6], (FF, D), FF ** -0.5, 0.09375, ((0, 16),))
    query_grad = bell_draw(streams_of[7], (D, FF), 1.0, 6.0, ((1, 16),), jnp.float32)
    return dict(noise_embed=noise_embed, action_embed=action_embed, prefix_kv=prefix_kv, flow_step=flow_step, action_mask=action_mask, w_up=w_up, w_down=w_down, query_grad=query_grad)


epsilon = 1e-06
sharpness_divisor = 6.0
damping_factor = 0.01

def attend(noise_embed, action_embed, prefix_kv, flow_step):
    demos = flow_step.shape[0]
    times = (flow_step.astype(jnp.float32) + 1.0) / (STEPS_T + 1.0)
    per_token = jnp.repeat(times, ACT)[:, None]
    noisy = noise_embed.astype(jnp.float32)
    clean = action_embed.astype(jnp.float32)
    inputs = per_token * noisy + (1.0 - per_token) * clean
    target = noisy - clean
    queries = inputs.reshape(demos, ACT, HEADS, CHANNEL_SPAN)
    probe_length = (queries * lax.rsqrt(lax.optimization_barrier(jnp.mean(queries * queries, -1, keepdims=True)) + epsilon)).astype(jnp.bfloat16)
    keys = prefix_kv[0].astype(jnp.float32)
    lookup_length = (keys * lax.rsqrt(lax.optimization_barrier(jnp.mean(keys * keys, -1, keepdims=True)) + epsilon)).astype(jnp.bfloat16)
    match_energies = jnp.einsum('zilf,zgf->zilg', probe_length.astype(jnp.float32), lookup_length.astype(jnp.float32)) * (sharpness_divisor / CHANNEL_SPAN)
    expo = jnp.exp(match_energies)
    weights = (expo / lax.optimization_barrier(jnp.sum(expo, -1, keepdims=True))).astype(jnp.bfloat16)
    mixed = jnp.einsum('dahp,dpe->dahe', weights.astype(jnp.float32), prefix_kv[1].astype(jnp.float32))
    hidden = inputs + mixed.reshape(demos * ACT, HEADS * CHANNEL_SPAN)
    normed_rows = (hidden * lax.rsqrt(lax.optimization_barrier(jnp.mean(hidden * hidden, -1, keepdims=True)) + epsilon)).astype(jnp.bfloat16)
    return (hidden, normed_rows, target)

def reference(noise_embed, action_embed, prefix_kv, flow_step, action_mask, w_up, w_down, query_grad):
    hidden, normed_rows, target = attend(noise_embed, action_embed, prefix_kv, flow_step)
    pre = jnp.dot(normed_rows, w_up, preferred_element_type=jnp.float32)
    sig = jax.nn.sigmoid(pre)
    slopes = sig * (1.0 + pre * (1.0 - sig))
    curves = sig * (1.0 - sig) * (2.0 + pre * (1.0 - 2.0 * sig))
    active = (pre * sig).astype(jnp.bfloat16)
    output = jnp.dot(active, w_down, preferred_element_type=jnp.float32)
    mask = action_mask.astype(jnp.float32)[:, None]
    err = (mask * (hidden + output - target)).astype(jnp.bfloat16)
    pulled = jnp.dot(err, w_down.T, preferred_element_type=jnp.float32)
    back = pulled * slopes

    def curvature(vector):
        direction_vector = jnp.dot(normed_rows, vector.astype(jnp.bfloat16), preferred_element_type=jnp.float32)
        linear = (slopes * direction_vector).astype(jnp.bfloat16)
        moved = jnp.dot(linear, w_down, preferred_element_type=jnp.float32)
        moved_err = (mask * moved).astype(jnp.bfloat16)
        second = (jnp.dot(moved_err, w_down.T, preferred_element_type=jnp.float32) * slopes + pulled * curves * direction_vector).astype(jnp.bfloat16)
        aggregate_total = lax.dot_general(normed_rows, second, (((0,), (0,)), ((), ())), preferred_element_type=jnp.float32)
        return aggregate_total / TOKENS
    vector = query_grad
    for step in range(ITERS):
        vector = query_grad + (1.0 - damping_factor) * vector - curvature(vector)
    projected = jnp.dot(normed_rows, vector.astype(jnp.bfloat16), preferred_element_type=jnp.float32)
    token_terms = lax.optimization_barrier(jnp.sum(projected * back, -1))
    scores = -lax.optimization_barrier(jnp.sum(token_terms.reshape(-1, ACT), -1)) / (ACT * math.sqrt(D * FF))
    return (vector, scores)
```

```python
import math

import jax
import jax.numpy as jnp
from jax import lax
from jax.sharding import Mesh
from jax.sharding import PartitionSpec as P

D = 1024
FF = 4096
STEPS_T = 10
ITERS = 2

epsilon = 1e-06
sharpness_divisor = 6.0
damping_factor = 0.01

AXES = ("zh", "y", "x", "zl", "c")
SIZES = (4, 4, 4, 4, 2)
GRID = ("x", "zl")


def attend(noise_embed, action_embed, prefix_kv, flow_step):
    demos = flow_step.shape[0]
    acts = noise_embed.shape[0] // demos
    channel_span = prefix_kv.shape[3]
    width = noise_embed.shape[1]
    times = (flow_step.astype(jnp.float32) + 1.0) / (STEPS_T + 1.0)
    per_token = jnp.repeat(times, acts)[:, None]
    noisy = noise_embed.astype(jnp.float32)
    clean = action_embed.astype(jnp.float32)
    inputs = per_token * noisy + (1.0 - per_token) * clean
    target = noisy - clean
    queries = inputs.reshape(demos, acts, width // channel_span, channel_span)
    probe_length = (
        queries * lax.rsqrt(jnp.mean(queries * queries, -1, keepdims=True) + epsilon)
    ).astype(jnp.bfloat16)
    keys = prefix_kv[0].astype(jnp.float32)
    lookup_length = (keys * lax.rsqrt(jnp.mean(keys * keys, -1, keepdims=True) + epsilon)).astype(
        jnp.bfloat16
    )
    match_energies = jnp.einsum(
        "zilf,zgf->zilg", probe_length, lookup_length, preferred_element_type=jnp.float32
    ) * (sharpness_divisor / channel_span)
    expo = jnp.exp(match_energies)
    weights = (expo / jnp.sum(expo, -1, keepdims=True)).astype(jnp.bfloat16)
    mixed = jnp.einsum("dahp,dpe->dahe", weights, prefix_kv[1], preferred_element_type=jnp.float32)
    hidden = inputs + mixed.reshape(demos * acts, width)
    normed_rows = (
        hidden * lax.rsqrt(jnp.mean(hidden * hidden, -1, keepdims=True) + epsilon)
    ).astype(jnp.bfloat16)
    return (hidden, normed_rows, target, acts)


def swap(blocks, axes):
    return lax.all_to_all(blocks, axes, 0, 0)


def collect(block, axes, members):
    return swap(jnp.broadcast_to(block[None], (members, *block.shape)), axes)


def total(blocks):
    return jnp.sum(blocks.astype(jnp.float32), 0)


def scatter_tokens(parts):
    parts = parts.astype(jnp.bfloat16)
    parts = parts.reshape(4, 4, *parts.shape[1:])
    stage = total(swap(jnp.swapaxes(parts, 0, 1), "y")).astype(jnp.bfloat16)
    return total(swap(stage, "zh"))


def gather_tokens(block):
    stage = collect(block, "zh", 4)
    full = jnp.swapaxes(collect(stage, "y", 4), 0, 1)
    return full.reshape(16, *block.shape)


def sum_copies(part):
    columns = part.shape[1]
    half = D // 2
    pair = total(swap(part.astype(jnp.bfloat16).reshape(2, half, columns), "c"))
    rows = total(swap(pair.astype(jnp.bfloat16).reshape(16, half // 16, columns), GRID))
    rows = collect(rows.astype(jnp.bfloat16), GRID, 16).reshape(half, columns)
    return collect(rows, "c", 2).reshape(D, columns)


def shards(noise_embed, action_embed, prefix_kv, flow_step, action_mask, w_up, w_down, query_grad):
    hidden, normed_rows, target, acts = attend(noise_embed, action_embed, prefix_kv, flow_step)
    tok_rows = normed_rows.shape[0]
    members = 16
    tokens = tok_rows * members
    mask_own = action_mask.astype(jnp.float32)[:, None]
    gathered = gather_tokens(normed_rows).reshape(tokens, D)

    def down(source):
        return jnp.dot(source, w_down, preferred_element_type=jnp.float32)

    def up(source):
        return jnp.dot(source, w_down.T, preferred_element_type=jnp.float32)

    def project(vector):
        return jnp.dot(gathered, vector.astype(jnp.bfloat16), preferred_element_type=jnp.float32)

    pre = jnp.dot(gathered, w_up, preferred_element_type=jnp.float32)
    sig = jax.nn.sigmoid(pre)
    slopes = sig * (1.0 + pre * (1.0 - sig))
    curves = sig * (1.0 - sig) * (2.0 + pre * (1.0 - 2.0 * sig))
    active = (pre * sig).astype(jnp.bfloat16)
    count = tokens * 32

    vector = query_grad
    pulled = None
    for step in range(ITERS):
        tangent = project(vector)
        linear = (slopes * tangent).astype(jnp.bfloat16)
        moved_part = down(linear).astype(jnp.bfloat16).reshape(members, tok_rows, D)
        if step == 0:
            out_part = down(active).astype(jnp.bfloat16).reshape(members, tok_rows, D)
            both = scatter_tokens(jnp.stack([out_part, moved_part], 1))
            err = (mask_own * (hidden + both[0] - target)).astype(jnp.bfloat16)
            moved_err = (mask_own * both[1]).astype(jnp.bfloat16)
            both = gather_tokens(jnp.stack([err, moved_err], 0))
            pulled = up(both[:, 0].reshape(tokens, D))
            moved_all = both[:, 1].reshape(tokens, D)
        else:
            moved = scatter_tokens(moved_part)
            moved_all = gather_tokens((mask_own * moved).astype(jnp.bfloat16)).reshape(tokens, D)
        second = (up(moved_all) * slopes + pulled * curves * tangent).astype(jnp.bfloat16)
        part = lax.dot_general(
            gathered, second, (((0,), (0,)), ((), ())), preferred_element_type=jnp.float32
        )
        product = sum_copies(part).astype(jnp.float32)
        vector = query_grad + (1.0 - damping_factor) * vector - product / count
    back = pulled * slopes
    token_terms = jnp.sum(project(vector) * back, -1)
    demo_terms = jnp.sum(token_terms.reshape(-1, acts), -1)
    owned = jnp.sum(swap(demo_terms.reshape(members, -1), ("zh", "y")), 0)
    return (vector, -owned / (acts * math.sqrt(D * FF)))


def solution(mesh):
    fine = Mesh(mesh.devices.reshape(SIZES), AXES)
    fsdp, everyone = AXES[:2], AXES
    placed = (
        P(everyone, None),
        P(everyone, None),
        P(None, everyone, None, None),
        P(everyone),
        P(everyone),
        P(None, fsdp),
        P(fsdp, None),
        P(None, fsdp),
    )
    return jax.shard_map(
        shards,
        mesh=fine,
        in_specs=placed,
        out_specs=(P(None, fsdp), P(everyone)),
        check_vma=False,
    )
```

```python
import math

import jax
import jax.numpy as jnp
from jax import lax
from jax.sharding import Mesh
from jax.sharding import PartitionSpec as P

D = 1024
FF = 4096
STEPS_T = 10

epsilon = 1e-06
sharpness_divisor = 6.0
damping_factor = 0.01

AXES = ("zh", "y", "x", "zl", "c")
SIZES = (4, 4, 4, 4, 2)
GRID = ("x", "zl")


def attend(noise_embed, action_embed, prefix_kv, flow_step):
    demos = flow_step.shape[0]
    acts = noise_embed.shape[0] // demos
    channel_span = prefix_kv.shape[3]
    width = noise_embed.shape[1]
    times = (flow_step.astype(jnp.float32) + 1.0) / (STEPS_T + 1.0)
    per_token = jnp.repeat(times, acts)[:, None]
    noisy = noise_embed.astype(jnp.float32)
    clean = action_embed.astype(jnp.float32)
    inputs = per_token * noisy + (1.0 - per_token) * clean
    target = noisy - clean
    queries = inputs.reshape(demos, acts, width // channel_span, channel_span)
    probe_length = (
        queries * lax.rsqrt(jnp.mean(queries * queries, -1, keepdims=True) + epsilon)
    ).astype(jnp.bfloat16)
    keys = prefix_kv[0].astype(jnp.float32)
    lookup_length = (keys * lax.rsqrt(jnp.mean(keys * keys, -1, keepdims=True) + epsilon)).astype(
        jnp.bfloat16
    )
    match_energies = jnp.einsum(
        "zilf,zgf->zilg", probe_length, lookup_length, preferred_element_type=jnp.float32
    ) * (sharpness_divisor / channel_span)
    expo = jnp.exp(match_energies)
    weights = (expo / jnp.sum(expo, -1, keepdims=True)).astype(jnp.bfloat16)
    mixed = jnp.einsum("dahp,dpe->dahe", weights, prefix_kv[1], preferred_element_type=jnp.float32)
    hidden = inputs + mixed.reshape(demos * acts, width)
    normed_rows = (
        hidden * lax.rsqrt(jnp.mean(hidden * hidden, -1, keepdims=True) + epsilon)
    ).astype(jnp.bfloat16)
    return (hidden, normed_rows, target, acts)


def swap(blocks, axes):
    return lax.all_to_all(blocks, axes, 0, 0)


def collect(block, axes, members):
    return swap(jnp.broadcast_to(block[None], (members, *block.shape)), axes)


def total(blocks):
    return jnp.sum(blocks.astype(jnp.float32), 0)


def sum_copies(part):
    columns = part.shape[1]
    half = D // 2
    pair = total(swap(part.astype(jnp.bfloat16).reshape(2, half, columns), "c"))
    rows = total(swap(pair.astype(jnp.bfloat16).reshape(16, half // 16, columns), GRID))
    rows = collect(rows.astype(jnp.bfloat16), GRID, 16).reshape(half, columns)
    return lax.all_gather(rows, "c", axis=0, tiled=True)


def shards(noise_embed, action_embed, prefix_kv, flow_step, action_mask, w_up, w_down, query_grad):
    hidden, normed_rows, target, acts = attend(noise_embed, action_embed, prefix_kv, flow_step)
    own = normed_rows.shape[0]
    tokens = own * 16
    count = tokens * 32
    mask_own = action_mask.astype(jnp.float32)[:, None]
    sent = normed_rows * action_mask.astype(jnp.bfloat16)[:, None]
    gathered = collect(collect(sent, "zh", 4), "y", 4).reshape(tokens, D)

    def down(source):
        return jnp.dot(source, w_down, preferred_element_type=jnp.float32).astype(jnp.bfloat16)

    def up(source):
        return jnp.dot(source, w_down.T, preferred_element_type=jnp.float32)

    def project(vector):
        return jnp.dot(gathered, vector.astype(jnp.bfloat16), preferred_element_type=jnp.float32)

    def hvp(second):
        part = lax.dot_general(
            gathered, second, (((0,), (0,)), ((), ())), preferred_element_type=jnp.float32
        )
        return sum_copies(part).astype(jnp.float32) / count

    units = w_up.shape[1]
    pre = jnp.dot(gathered, w_up, preferred_element_type=jnp.float32)
    sig = jax.nn.sigmoid(pre)
    slopes = sig * (1.0 + pre * (1.0 - sig))
    curves = sig * (1.0 - sig) * (2.0 + pre * (1.0 - 2.0 * sig))
    active = (pre * sig).astype(jnp.bfloat16)
    tangent = project(query_grad)
    linear = (slopes * tangent).astype(jnp.bfloat16)
    source = jnp.stack([active.reshape(16, own, units), linear.reshape(16, own, units)], 1)
    parts = down(source.reshape(2 * tokens, units)).reshape(4, 4, 2, own, D)
    stage = total(swap(parts, "y")).astype(jnp.bfloat16)
    both = total(swap(stage, "zh"))
    err = (mask_own * (hidden + both[0] - target)).astype(jnp.bfloat16)
    moved_err = (mask_own * both[1]).astype(jnp.bfloat16)
    both = lax.all_gather(jnp.stack([err, moved_err], 0), "zh", axis=0)
    both = up(collect(both, "y", 4).reshape(2 * tokens, D)).reshape(16, 2, own, units)
    pulled = both[:, 0].reshape(tokens, units)
    moved = both[:, 1].reshape(tokens, units)
    bend = pulled * curves
    vector = query_grad + (1.0 - damping_factor) * query_grad
    vector = vector - hvp((moved * slopes + bend * tangent).astype(jnp.bfloat16))

    tangent = project(vector)
    parts = down((slopes * tangent).astype(jnp.bfloat16)).reshape(4, 4 * own, D)
    stage = total(swap(parts, "y")).astype(jnp.bfloat16)
    stage = total(lax.all_gather(stage, "zh", axis=0)).astype(jnp.bfloat16)
    moved = up(collect(stage, "y", 4).reshape(tokens, D))
    vector = query_grad + (1.0 - damping_factor) * vector
    vector = vector - hvp((moved * slopes + bend * tangent).astype(jnp.bfloat16))

    token_terms = jnp.sum(project(vector) * (pulled * slopes), -1)
    demo_terms = jnp.sum(token_terms.reshape(-1, acts), -1)
    owned = jnp.sum(swap(demo_terms.reshape(16, -1), ("y", "zh")), 0)
    return (vector, -owned / (acts * math.sqrt(D * FF)))


def solution(mesh):
    fine = Mesh(mesh.devices.reshape(SIZES), AXES)
    fsdp, everyone = AXES[:2], AXES
    placed = (
        P(everyone, None),
        P(everyone, None),
        P(None, everyone, None, None),
        P(everyone),
        P(everyone),
        P(None, fsdp),
        P(fsdp, None),
        P(None, fsdp),
    )
    return jax.shard_map(
        shards,
        mesh=fine,
        in_specs=placed,
        out_specs=(P(None, fsdp), P(everyone)),
        check_vma=False,
    )
```

```python
import math

import jax
import jax.numpy as jnp
from jax import lax
from jax.sharding import Mesh
from jax.sharding import PartitionSpec as P

D = 1024
FF = 4096
STEPS_T = 10

epsilon = 1e-06
sharpness_divisor = 6.0
damping_factor = 0.01

AXES = ("zh", "y", "x", "zl", "c")
SIZES = (4, 4, 4, 4, 2)
GRID = ("x", "zl")


def attend(noise_embed, action_embed, prefix_kv, flow_step):
    demos = flow_step.shape[0]
    acts = noise_embed.shape[0] // demos
    channel_span = prefix_kv.shape[3]
    width = noise_embed.shape[1]
    times = (flow_step.astype(jnp.float32) + 1.0) / (STEPS_T + 1.0)
    per_token = jnp.repeat(times, acts)[:, None]
    noisy = noise_embed.astype(jnp.float32)
    clean = action_embed.astype(jnp.float32)
    inputs = per_token * noisy + (1.0 - per_token) * clean
    target = noisy - clean
    queries = inputs.reshape(demos, acts, width // channel_span, channel_span)
    probe_length = (
        queries * lax.rsqrt(jnp.mean(queries * queries, -1, keepdims=True) + epsilon)
    ).astype(jnp.bfloat16)
    keys = prefix_kv[0].astype(jnp.float32)
    lookup_length = (keys * lax.rsqrt(jnp.mean(keys * keys, -1, keepdims=True) + epsilon)).astype(
        jnp.bfloat16
    )
    match_energies = jnp.einsum(
        "zilf,zgf->zilg", probe_length, lookup_length, preferred_element_type=jnp.float32
    ) * (sharpness_divisor / channel_span)
    expo = jnp.exp(match_energies)
    weights = (expo / jnp.sum(expo, -1, keepdims=True)).astype(jnp.bfloat16)
    mixed = jnp.einsum("dahp,dpe->dahe", weights, prefix_kv[1], preferred_element_type=jnp.float32)
    hidden = inputs + mixed.reshape(demos * acts, width)
    normed_rows = (
        hidden * lax.rsqrt(jnp.mean(hidden * hidden, -1, keepdims=True) + epsilon)
    ).astype(jnp.bfloat16)
    return (hidden, normed_rows, target, acts)


def swap(blocks, axes):
    return lax.all_to_all(blocks, axes, 0, 0)


def collect(block, axes, members):
    return swap(jnp.broadcast_to(block[None], (members, *block.shape)), axes)


def total(blocks):
    return jnp.sum(blocks.astype(jnp.float32), 0)


def sum_copies(kept, given):
    half, columns = kept.shape
    taken = lax.ppermute(given.astype(jnp.bfloat16), "c", [(0, 1), (1, 0)])
    pair = (kept + taken.astype(jnp.float32)).astype(jnp.bfloat16)
    rows = total(swap(pair.reshape(16, half // 16, columns), GRID))
    rows = collect(rows.astype(jnp.bfloat16), GRID, 16).reshape(half, columns)
    return lax.all_gather(rows, "c", axis=0, tiled=True)


def shards(noise_embed, action_embed, prefix_kv, flow_step, action_mask, w_up, w_down, query_grad):
    hidden, normed_rows, target, acts = attend(noise_embed, action_embed, prefix_kv, flow_step)
    own = normed_rows.shape[0]
    tokens = own * 16
    count = tokens * 32
    mask_own = action_mask.astype(jnp.float32)[:, None]
    sent = normed_rows * action_mask.astype(jnp.bfloat16)[:, None]
    gathered = collect(collect(sent, "zh", 4), "y", 4).reshape(tokens, D)

    def down(source):
        return jnp.dot(source, w_down, preferred_element_type=jnp.float32).astype(jnp.bfloat16)

    def up(source):
        return jnp.dot(source, w_down.T, preferred_element_type=jnp.float32)

    def project(vector):
        return jnp.dot(gathered, vector.astype(jnp.bfloat16), preferred_element_type=jnp.float32)

    core = lax.axis_index("c")
    mine = lax.dynamic_slice_in_dim(gathered, core * (D // 2), D // 2, 1)
    other = lax.dynamic_slice_in_dim(gathered, (1 - core) * (D // 2), D // 2, 1)

    def outer(features, second):
        return lax.dot_general(
            features, second, (((0,), (0,)), ((), ())), preferred_element_type=jnp.float32
        )

    def hvp(second):
        return sum_copies(outer(mine, second), outer(other, second)).astype(jnp.float32) / count

    units = w_up.shape[1]
    pre = jnp.dot(gathered, w_up, preferred_element_type=jnp.float32)
    sig = jax.nn.sigmoid(pre)
    slopes = sig * (1.0 + pre * (1.0 - sig))
    curves = sig * (1.0 - sig) * (2.0 + pre * (1.0 - 2.0 * sig))
    active = (pre * sig).astype(jnp.bfloat16)
    tangent = project(query_grad)
    linear = (slopes * tangent).astype(jnp.bfloat16)
    source = jnp.stack([active.reshape(16, own, units), linear.reshape(16, own, units)], 1)
    parts = down(source.reshape(2 * tokens, units)).reshape(4, 4, 2, own, D)
    stage = total(swap(parts, "y")).astype(jnp.bfloat16)
    both = total(swap(stage, "zh"))
    err = (mask_own * (hidden + both[0] - target)).astype(jnp.bfloat16)
    moved_err = (mask_own * both[1]).astype(jnp.bfloat16)
    both = lax.all_gather(jnp.stack([err, moved_err], 0), "zh", axis=0)
    both = up(collect(both, "y", 4).reshape(2 * tokens, D)).reshape(16, 2, own, units)
    pulled = both[:, 0].reshape(tokens, units)
    moved = both[:, 1].reshape(tokens, units)
    bend = pulled * curves
    vector = query_grad + (1.0 - damping_factor) * query_grad
    vector = vector - hvp((moved * slopes + bend * tangent).astype(jnp.bfloat16))

    tangent = project(vector)
    parts = down((slopes * tangent).astype(jnp.bfloat16)).reshape(4, 4 * own, D)
    stage = total(swap(parts, "y")).astype(jnp.bfloat16)
    stage = total(lax.all_gather(stage, "zh", axis=0)).astype(jnp.bfloat16)
    moved = up(collect(stage, "y", 4).reshape(tokens, D))
    vector = query_grad + (1.0 - damping_factor) * vector
    vector = vector - hvp((moved * slopes + bend * tangent).astype(jnp.bfloat16))

    token_terms = jnp.sum(project(vector) * (pulled * slopes), -1)
    demo_terms = jnp.sum(token_terms.reshape(-1, acts), -1)
    owned = jnp.sum(swap(demo_terms.reshape(16, -1), ("y", "zh")), 0)
    return (vector, -owned / (acts * math.sqrt(D * FF)))


def solution(mesh):
    fine = Mesh(mesh.devices.reshape(SIZES), AXES)
    fsdp, everyone = AXES[:2], AXES
    placed = (
        P(everyone, None),
        P(everyone, None),
        P(None, everyone, None, None),
        P(everyone),
        P(everyone),
        P(None, fsdp),
        P(fsdp, None),
        P(None, fsdp),
    )
    return jax.shard_map(
        shards,
        mesh=fine,
        in_specs=placed,
        out_specs=(P(None, fsdp), P(everyone)),
        check_vma=False,
    )
```

```python
import functools
import math

import jax
import jax.numpy as jnp
from jax import lax
from jax.experimental import pallas as pl
from jax.experimental.pallas import tpu as pltpu
from jax.sharding import Mesh
from jax.sharding import PartitionSpec as P

D = 1024
FF = 4096
STEPS_T = 10
TOKENS = 8192

epsilon = 1e-06
sharpness_divisor = 6.0
damping_factor = 0.01
rest = 1.0 - damping_factor
keep = 1.0 + rest

AXES = ("zh", "y", "x", "zl", "c")
SIZES = (4, 4, 4, 4, 2)
GRID = ("x", "zl")

SCALARS = pl.BlockSpec(memory_space=pltpu.SMEM)
BLOCK = pl.BlockSpec(memory_space=pltpu.VMEM)


def local(kernel, specs, outs):
    return pl.pallas_call(
        kernel,
        in_specs=specs,
        out_specs=[BLOCK] * len(outs),
        out_shape=[jax.ShapeDtypeStruct(shape, dtype) for shape, dtype in outs],
        compiler_params=pltpu.CompilerParams(vmem_limit_bytes=24 * 2**20),
    )


def nn(left, right):
    return jnp.dot(left, right, preferred_element_type=jnp.float32)


def nt(left, right):
    return lax.dot_general(
        left, right, (((1,), (1,)), ((), ())), preferred_element_type=jnp.float32
    )


def tn(left, right):
    return lax.dot_general(
        left, right, (((0,), (0,)), ((), ())), preferred_element_type=jnp.float32
    )


def attend(flow_ref, mask_ref, noise_ref, action_ref, kv_ref, sent_ref, resid_ref):
    acts, width = noise_ref.shape
    span = kv_ref.shape[3]
    heads = width // span
    time = (flow_ref[0].astype(jnp.float32) + 1.0) / (STEPS_T + 1.0)
    row = lax.broadcasted_iota(jnp.int32, (acts, 128), 0)
    mask = jnp.zeros((acts, 128), jnp.float32)
    for i in range(acts):
        mask = jnp.where(row == i, mask_ref[i].astype(jnp.float32), mask)
    mask = mask[:, :1]
    noisy = noise_ref[...].astype(jnp.float32)
    clean = action_ref[...].astype(jnp.float32)
    inputs = time * noisy + (1.0 - time) * clean
    queries = jnp.concatenate([inputs[:, i * span : (i + 1) * span] for i in range(heads)], 0)
    queries = queries * lax.rsqrt(jnp.mean(queries * queries, -1, keepdims=True) + epsilon)
    keys = kv_ref[0, 0].astype(jnp.float32)
    keys = keys * lax.rsqrt(jnp.mean(keys * keys, -1, keepdims=True) + epsilon)
    energies = nt(queries.astype(jnp.bfloat16), keys.astype(jnp.bfloat16))
    expo = jnp.exp(energies * (sharpness_divisor / span))
    weights = (expo / jnp.sum(expo, -1, keepdims=True)).astype(jnp.bfloat16)
    mixed = nn(weights, kv_ref[1, 0])
    mixed = jnp.concatenate([mixed[i * acts : (i + 1) * acts] for i in range(heads)], 1)
    hidden = inputs + mixed
    normed = hidden * lax.rsqrt(jnp.mean(hidden * hidden, -1, keepdims=True) + epsilon)
    normed = (normed.astype(jnp.bfloat16).astype(jnp.float32) * mask).astype(jnp.bfloat16)
    for i in range(sent_ref.shape[0]):
        sent_ref[i] = normed
    resid_ref[...] = mask * (hidden - (noisy - clean))


def forward(rows_ref, up_ref, query_ref, lin_ref, slopes_ref, curves_ref, tangent_ref):
    rows = rows_ref[...]
    pre = nn(rows, up_ref[...])
    sig = jax.nn.sigmoid(pre)
    slopes = sig * (1.0 + pre * (1.0 - sig))
    curves_ref[...] = sig * (1.0 - sig) * (2.0 + pre * (1.0 - 2.0 * sig))
    tangent = nn(rows, query_ref[...].astype(jnp.bfloat16))
    slopes_ref[...] = slopes
    tangent_ref[...] = tangent
    active = (pre * sig).astype(jnp.bfloat16)
    linear = (slopes * tangent).astype(jnp.bfloat16)
    lin_ref[:, :, 0] = active.reshape(4, 4, 16, -1)
    lin_ref[:, :, 1] = linear.reshape(4, 4, 16, -1)


def down(lin_ref, *refs):
    *blocks, out_ref = refs
    place = lax.axis_index("y")
    rows = out_ref.shape[0]
    out = 0.0
    for j, block in enumerate(blocks):
        source = lin_ref[lax.rem(place + j, 4)].reshape(rows, -1)
        out = out + nn(source, block[...])
    out_ref[...] = out.astype(jnp.bfloat16)


def pull(source_ref, *refs):
    *blocks, out_ref = refs
    place = lax.axis_index("y")
    if source_ref.ndim == 3:
        source = source_ref[0].astype(jnp.float32)
        for i in range(1, source_ref.shape[0]):
            source = source + source_ref[i].astype(jnp.float32)
        source = source.astype(jnp.bfloat16)
    else:
        source = source_ref[...]
    for j, block in enumerate(blocks):
        out_ref[lax.rem(place + j, 4)] = nt(source, block[...]).astype(jnp.bfloat16)


def halves(rows_ref, second, kept_ref, given_ref):
    half = D // 2
    low = tn(rows_ref[:, :half], second).astype(jnp.bfloat16)
    high = tn(rows_ref[:, half:], second).astype(jnp.bfloat16)
    core = lax.axis_index("c")

    @pl.when(core == 0)
    def _():
        kept_ref[...] = low
        given_ref[...] = high

    @pl.when(core == 1)
    def _():
        kept_ref[...] = high
        given_ref[...] = low


def curve_first(
    both_ref, slopes_ref, curves_ref, tangent_ref, rows_ref, kept_ref, given_ref, bend_ref, back_ref
):
    shape = slopes_ref.shape
    pulled = both_ref[:, :, 0].reshape(shape).astype(jnp.float32)
    moved = both_ref[:, :, 1].reshape(shape).astype(jnp.float32)
    slopes = slopes_ref[...]
    bend = pulled * curves_ref[...]
    bend_ref[...] = bend
    back_ref[...] = pulled * slopes
    second = (moved * slopes + bend * tangent_ref[...]).astype(jnp.bfloat16)
    halves(rows_ref, second, kept_ref, given_ref)


def turn(rows_ref, first_ref, slopes_ref, tangent_ref, lin_ref, along_ref):
    along = nn(rows_ref[...], first_ref[...]) / TOKENS
    along_ref[...] = along
    later = keep * tangent_ref[...] - along
    lin_ref[...] = (slopes_ref[...] * later).astype(jnp.bfloat16).reshape(lin_ref.shape)


def curve_second(
    moved_ref, slopes_ref, bend_ref, tangent_ref, along_ref, rows_ref, kept_ref, given_ref
):
    moved = moved_ref[...].reshape(slopes_ref.shape).astype(jnp.float32)
    later = keep * tangent_ref[...] - along_ref[...]
    second = (moved * slopes_ref[...] + bend_ref[...] * later).astype(jnp.bfloat16)
    halves(rows_ref, second, kept_ref, given_ref)


def score(rows_ref, second_ref, tangent_ref, along_ref, back_ref, terms_ref):
    along = nn(rows_ref[...], second_ref[...]) / TOKENS
    projected = (1.0 + rest * keep) * tangent_ref[...] - rest * along_ref[...] - along
    terms = (projected * back_ref[...]).reshape(16, 2, 8, 256)
    terms = terms[:, 0] + terms[:, 1]
    terms_ref[...] = terms[:, :, :128] + terms[:, :, 128:]


def swap(blocks, axes):
    return lax.all_to_all(blocks, axes, 0, 0)


def collect(block, axes, members):
    return swap(jnp.broadcast_to(block[None], (members, *block.shape)), axes)


def total(blocks):
    return jnp.sum(blocks.astype(jnp.float32), 0)


def sum_copies(kept, given):
    half, columns = kept.shape
    taken = lax.ppermute(given, "c", [(0, 1), (1, 0)])
    pair = (kept.astype(jnp.float32) + taken.astype(jnp.float32)).astype(jnp.bfloat16)
    rows = total(swap(pair.reshape(16, half // 16, columns), GRID))
    rows = collect(rows.astype(jnp.bfloat16), GRID, 16).reshape(half, columns)
    return lax.all_gather(rows, "c", axis=0, tiled=True)


def shards(noise_embed, action_embed, prefix_kv, flow_step, action_mask, w_up, w_down, query_grad):
    own = noise_embed.shape[0]
    tokens = own * 16
    units = w_up.shape[1]
    half = jnp.bfloat16
    full = jnp.float32
    square = ((tokens, units), full)
    blocks = [w_down]
    for shift in (1, 2, 3):
        blocks.append(lax.ppermute(w_down, "y", [((i + shift) % 4, i) for i in range(4)]))

    sent, resid = local(
        attend,
        [SCALARS, SCALARS, BLOCK, BLOCK, BLOCK],
        [((4, own, D), half), ((own, D), full)],
    )(flow_step, action_mask, noise_embed, action_embed, prefix_kv)
    stage, blocks = lax.optimization_barrier((swap(sent, "zh"), blocks))
    rows = collect(stage, "y", 4).reshape(tokens, D)
    lin, slopes, curves, tangent = local(
        forward, [BLOCK] * 3, [((4, 4, 2, own, units), half), square, square, square]
    )(rows, w_up, query_grad)
    (stage,) = local(down, [BLOCK] * 5, [((8 * own, D), half)])(swap(lin, "y"), *blocks)
    both = total(swap(stage.reshape(4, 2, own, D), "zh"))
    both = jnp.stack([(resid + both[0]).astype(half), both[1].astype(half)])
    both = lax.all_gather(both, "zh", axis=0).reshape(8 * own, D)
    (both,) = local(pull, [BLOCK] * 5, [((4, 8 * own, units), half)])(both, *blocks)
    both = swap(both, "y").reshape(4, 4, 2, own, units)
    sides = [((D // 2, units), half)] * 2
    kept, given, bend, back = local(curve_first, [BLOCK] * 5, [*sides, square, square])(
        both, slopes, curves, tangent, rows
    )
    first = sum_copies(kept, given)

    lin, along = local(turn, [BLOCK] * 4, [((4, 4 * own, units), half), square])(
        rows, first, slopes, tangent
    )
    (stage,) = local(down, [BLOCK] * 5, [((4 * own, D), half)])(swap(lin, "y"), *blocks)
    stage = lax.all_gather(stage, "zh", axis=0)
    (moved,) = local(pull, [BLOCK] * 5, [((4, 4 * own, units), half)])(stage, *blocks)
    kept, given = local(curve_second, [BLOCK] * 6, sides)(
        swap(moved, "y"), slopes, bend, tangent, along, rows
    )
    second = sum_copies(kept, given)

    (terms,) = local(score, [BLOCK] * 5, [((16, 8, 128), full)])(
        rows, second, tangent, along, back
    )
    owned = jnp.sum(swap(terms, ("y", "zh"))).reshape(1)
    vector = (1.0 + rest * keep) * query_grad - (
        rest * first.astype(full) + second.astype(full)
    ) / TOKENS
    return (vector, -owned / (own * math.sqrt(D * FF)))


def solution(mesh):
    fine = Mesh(mesh.devices.reshape(SIZES), AXES)
    fsdp, everyone = AXES[:2], AXES
    placed = (
        P(everyone, None),
        P(everyone, None),
        P(None, everyone, None, None),
        P(everyone),
        P(everyone),
        P(None, fsdp),
        P(fsdp, None),
        P(None, fsdp),
    )
    return jax.shard_map(
        shards,
        mesh=fine,
        in_specs=placed,
        out_specs=(P(None, fsdp), P(everyone)),
        check_vma=False,
    )
```

```python
import functools
import math

import jax
import jax.numpy as jnp
from jax import lax
from jax.experimental import pallas as pl
from jax.experimental.pallas import tpu as pltpu
from jax.sharding import Mesh
from jax.sharding import PartitionSpec as P

D = 1024
FF = 4096
STEPS_T = 10
TOKENS = 8192

epsilon = 1e-06
sharpness_divisor = 6.0
damping_factor = 0.01
rest = 1.0 - damping_factor
keep = 1.0 + rest

AXES = ("zh", "y", "x", "zl", "c")
SIZES = (4, 4, 4, 4, 2)
GRID = ("x", "zl")

SCALARS = pl.BlockSpec(memory_space=pltpu.SMEM)
BLOCK = pl.BlockSpec(memory_space=pltpu.VMEM)


FAR = pl.BlockSpec(memory_space=pltpu.HBM)


def local(kernel, specs, outs, out_specs=None, scratch=()):
    return pl.pallas_call(
        kernel,
        in_specs=specs,
        out_specs=out_specs or [BLOCK] * len(outs),
        scratch_shapes=scratch,
        out_shape=[jax.ShapeDtypeStruct(shape, dtype) for shape, dtype in outs],
        compiler_params=pltpu.CompilerParams(vmem_limit_bytes=24 * 2**20),
    )


def nn(left, right):
    return jnp.dot(left, right, preferred_element_type=jnp.float32)


def nt(left, right):
    return lax.dot_general(
        left, right, (((1,), (1,)), ((), ())), preferred_element_type=jnp.float32
    )


def tn(left, right):
    return lax.dot_general(
        left, right, (((0,), (0,)), ((), ())), preferred_element_type=jnp.float32
    )


def attend(
    flow_ref, mask_ref, noise_far, action_far, kv_far, sent_ref, resid_ref,
    noise_ref, action_ref, kv_ref, sems,
):
    copies = [
        pltpu.make_async_copy(far, near, sems.at[i])
        for i, (far, near) in enumerate(
            ((kv_far, kv_ref), (noise_far, noise_ref), (action_far, action_ref))
        )
    ]
    for copy in copies:
        copy.start()
    for copy in copies:
        copy.wait()
    acts, width = noise_ref.shape
    span = kv_ref.shape[3]
    heads = width // span
    time = (flow_ref[0].astype(jnp.float32) + 1.0) / (STEPS_T + 1.0)
    row = lax.broadcasted_iota(jnp.int32, (acts, 128), 0)
    mask = jnp.zeros((acts, 128), jnp.float32)
    for i in range(acts):
        mask = jnp.where(row == i, mask_ref[i].astype(jnp.float32), mask)
    mask = mask[:, :1]
    noisy = noise_ref[...].astype(jnp.float32)
    clean = action_ref[...].astype(jnp.float32)
    inputs = time * noisy + (1.0 - time) * clean
    queries = jnp.concatenate([inputs[:, i * span : (i + 1) * span] for i in range(heads)], 0)
    queries = queries * lax.rsqrt(jnp.mean(queries * queries, -1, keepdims=True) + epsilon)
    keys = kv_ref[0, 0].astype(jnp.float32)
    keys = keys * lax.rsqrt(jnp.mean(keys * keys, -1, keepdims=True) + epsilon)
    energies = nt(queries.astype(jnp.bfloat16), keys.astype(jnp.bfloat16))
    expo = jnp.exp(energies * (sharpness_divisor / span))
    weights = (expo / jnp.sum(expo, -1, keepdims=True)).astype(jnp.bfloat16)
    mixed = nn(weights, kv_ref[1, 0])
    mixed = jnp.concatenate([mixed[i * acts : (i + 1) * acts] for i in range(heads)], 1)
    hidden = inputs + mixed
    normed = hidden * lax.rsqrt(jnp.mean(hidden * hidden, -1, keepdims=True) + epsilon)
    normed = (normed.astype(jnp.bfloat16).astype(jnp.float32) * mask).astype(jnp.bfloat16)
    for i in range(sent_ref.shape[0]):
        sent_ref[i] = normed
    resid_ref[...] = mask * (hidden - (noisy - clean))


def forward(rows_ref, up_ref, query_ref, lin_ref, slopes_ref, curves_ref, tangent_ref):
    rows = rows_ref[...]
    pre = nn(rows, up_ref[...])
    sig = jax.nn.sigmoid(pre)
    slopes = sig * (1.0 + pre * (1.0 - sig))
    curves_ref[...] = sig * (1.0 - sig) * (2.0 + pre * (1.0 - 2.0 * sig))
    tangent = nn(rows, query_ref[...].astype(jnp.bfloat16))
    slopes_ref[...] = slopes
    tangent_ref[...] = tangent
    active = (pre * sig).astype(jnp.bfloat16)
    linear = (slopes * tangent).astype(jnp.bfloat16)
    lin_ref[:, :, 0] = active.reshape(4, 4, 16, -1)
    lin_ref[:, :, 1] = linear.reshape(4, 4, 16, -1)


def down(lin_ref, *refs):
    *blocks, out_ref = refs
    place = lax.axis_index("y")
    rows = out_ref.shape[0]
    out = 0.0
    for j, block in enumerate(blocks):
        source = lin_ref[lax.rem(place + j, 4)].reshape(rows, -1)
        out = out + nn(source, block[...])
    out_ref[...] = out.astype(jnp.bfloat16)


def pull(source_ref, *refs):
    *blocks, out_ref = refs
    place = lax.axis_index("y")
    if source_ref.ndim == 3:
        source = source_ref[0].astype(jnp.float32)
        for i in range(1, source_ref.shape[0]):
            source = source + source_ref[i].astype(jnp.float32)
        source = source.astype(jnp.bfloat16)
    else:
        source = source_ref[...]
    for j, block in enumerate(blocks):
        out_ref[lax.rem(place + j, 4)] = nt(source, block[...]).astype(jnp.bfloat16)


def halves(rows_ref, second, kept_ref, given_ref):
    half = D // 2
    low = tn(rows_ref[:, :half], second).astype(jnp.bfloat16)
    high = tn(rows_ref[:, half:], second).astype(jnp.bfloat16)
    core = lax.axis_index("c")

    @pl.when(core == 0)
    def _():
        kept_ref[...] = low
        given_ref[...] = high

    @pl.when(core == 1)
    def _():
        kept_ref[...] = high
        given_ref[...] = low


def curve_first(
    both_ref, slopes_ref, curves_ref, tangent_ref, rows_ref, kept_ref, given_ref, bend_ref, back_ref
):
    shape = slopes_ref.shape
    pulled = both_ref[:, :, 0].reshape(shape).astype(jnp.float32)
    moved = both_ref[:, :, 1].reshape(shape).astype(jnp.float32)
    slopes = slopes_ref[...]
    bend = pulled * curves_ref[...]
    bend_ref[...] = bend
    back_ref[...] = pulled * slopes
    second = (moved * slopes + bend * tangent_ref[...]).astype(jnp.bfloat16)
    halves(rows_ref, second, kept_ref, given_ref)


def turn(rows_ref, first_ref, slopes_ref, tangent_ref, lin_ref, along_ref):
    along = nn(rows_ref[...], first_ref[...]) / TOKENS
    along_ref[...] = along
    later = keep * tangent_ref[...] - along
    lin_ref[...] = (slopes_ref[...] * later).astype(jnp.bfloat16).reshape(lin_ref.shape)


def curve_second(
    moved_ref, slopes_ref, bend_ref, tangent_ref, along_ref, rows_ref, kept_ref, given_ref
):
    moved = moved_ref[...].reshape(slopes_ref.shape).astype(jnp.float32)
    later = keep * tangent_ref[...] - along_ref[...]
    second = (moved * slopes_ref[...] + bend_ref[...] * later).astype(jnp.bfloat16)
    halves(rows_ref, second, kept_ref, given_ref)


def score(
    rows_ref, second_ref, tangent_ref, along_ref, back_ref, first_ref, query_ref,
    terms_ref, vector_far, vector_ref, sem,
):
    first = first_ref[...].astype(jnp.float32)
    second = second_ref[...].astype(jnp.float32)
    vector_ref[...] = (1.0 + rest * keep) * query_ref[...] - (rest * first + second) / TOKENS
    copy = pltpu.make_async_copy(vector_ref, vector_far, sem)
    copy.start()
    along = nn(rows_ref[...], second_ref[...]) / TOKENS
    projected = (1.0 + rest * keep) * tangent_ref[...] - rest * along_ref[...] - along
    terms = (projected * back_ref[...]).reshape(16, 16, 256)
    terms = jnp.sum(terms[:, :, :128] + terms[:, :, 128:], 1, keepdims=True)
    terms_ref[...] = terms
    copy.wait()


def finish(terms_ref, score_ref):
    acts = TOKENS // 512
    score_ref[0] = -jnp.sum(terms_ref[...]) / (acts * math.sqrt(D * FF))


def swap(blocks, axes):
    return lax.all_to_all(blocks, axes, 0, 0)


def collect(block, axes, members):
    return swap(jnp.broadcast_to(block[None], (members, *block.shape)), axes)


def total(blocks):
    return jnp.sum(blocks.astype(jnp.float32), 0)


def sum_copies(kept, given):
    half, columns = kept.shape
    taken = lax.ppermute(given, "c", [(0, 1), (1, 0)])
    pair = (kept.astype(jnp.float32) + taken.astype(jnp.float32)).astype(jnp.bfloat16)
    rows = total(swap(pair.reshape(16, half // 16, columns), GRID))
    rows = collect(rows.astype(jnp.bfloat16), GRID, 16).reshape(half, columns)
    return lax.all_gather(rows, "c", axis=0, tiled=True)


def shards(noise_embed, action_embed, prefix_kv, flow_step, action_mask, w_up, w_down, query_grad):
    own = noise_embed.shape[0]
    tokens = own * 16
    units = w_up.shape[1]
    half = jnp.bfloat16
    full = jnp.float32
    square = ((tokens, units), full)
    blocks = [w_down]
    for shift in (1, 2, 3):
        blocks.append(lax.ppermute(w_down, "y", [((i + shift) % 4, i) for i in range(4)]))

    sent, resid = local(
        attend,
        [SCALARS, SCALARS, FAR, FAR, FAR],
        [((4, own, D), half), ((own, D), full)],
        scratch=[
            pltpu.VMEM(noise_embed.shape, half),
            pltpu.VMEM(action_embed.shape, half),
            pltpu.VMEM(prefix_kv.shape, half),
            pltpu.SemaphoreType.DMA((3,)),
        ],
    )(flow_step, action_mask, noise_embed, action_embed, prefix_kv)
    stage, blocks = lax.optimization_barrier((swap(sent, "zh"), blocks))
    rows = collect(stage, "y", 4).reshape(tokens, D)
    lin, slopes, curves, tangent = local(
        forward, [BLOCK] * 3, [((4, 4, 2, own, units), half), square, square, square]
    )(rows, w_up, query_grad)
    (stage,) = local(down, [BLOCK] * 5, [((8 * own, D), half)])(swap(lin, "y"), *blocks)
    both = total(swap(stage.reshape(4, 2, own, D), "zh"))
    both = jnp.stack([(resid + both[0]).astype(half), both[1].astype(half)])
    both = collect(both, "zh", 4).reshape(8 * own, D)
    (both,) = local(pull, [BLOCK] * 5, [((4, 8 * own, units), half)])(both, *blocks)
    both = swap(both, "y").reshape(4, 4, 2, own, units)
    sides = [((D // 2, units), half)] * 2
    kept, given, bend, back = local(curve_first, [BLOCK] * 5, [*sides, square, square])(
        both, slopes, curves, tangent, rows
    )
    first = sum_copies(kept, given)

    lin, along = local(turn, [BLOCK] * 4, [((4, 4 * own, units), half), square])(
        rows, first, slopes, tangent
    )
    (stage,) = local(down, [BLOCK] * 5, [((4 * own, D), half)])(swap(lin, "y"), *blocks)
    stage = lax.all_gather(stage, "zh", axis=0)
    (moved,) = local(pull, [BLOCK] * 5, [((4, 4 * own, units), half)])(stage, *blocks)
    kept, given = local(curve_second, [BLOCK] * 6, sides)(
        swap(moved, "y"), slopes, bend, tangent, along, rows
    )
    second = sum_copies(kept, given)

    terms, vector = local(
        score,
        [BLOCK] * 7,
        [((16, 1, 128), full), (query_grad.shape, full)],
        [BLOCK, FAR],
        [pltpu.VMEM(query_grad.shape, full), pltpu.SemaphoreType.DMA],
    )(rows, second, tangent, along, back, first, query_grad)
    (owned,) = local(finish, [BLOCK], [((1,), full)], [SCALARS])(swap(terms, ("y", "zh")))
    return (vector, owned)


def solution(mesh):
    fine = Mesh(mesh.devices.reshape(SIZES), AXES)
    fsdp, everyone = AXES[:2], AXES
    placed = (
        P(everyone, None),
        P(everyone, None),
        P(None, everyone, None, None),
        P(everyone),
        P(everyone),
        P(None, fsdp),
        P(fsdp, None),
        P(None, fsdp),
    )
    return jax.shard_map(
        shards,
        mesh=fine,
        in_specs=placed,
        out_specs=(P(None, fsdp), P(everyone)),
        check_vma=False,
    )
```

```python
import functools
import math

import jax
import jax.numpy as jnp
from jax import lax
from jax.experimental import pallas as pl
from jax.experimental.pallas import tpu as pltpu
from jax.sharding import Mesh
from jax.sharding import PartitionSpec as P

D = 1024
FF = 4096
STEPS_T = 10
TOKENS = 8192

epsilon = 1e-06
sharpness_divisor = 6.0
damping_factor = 0.01
rest = 1.0 - damping_factor
keep = 1.0 + rest

AXES = ("zh", "y", "x", "zl", "c")
SIZES = (4, 4, 4, 4, 2)
GRID = ("x", "zl")

SCALARS = pl.BlockSpec(memory_space=pltpu.SMEM)
BLOCK = pl.BlockSpec(memory_space=pltpu.VMEM)


FAR = pl.BlockSpec(memory_space=pltpu.HBM)


def local(kernel, specs, outs, out_specs=None, scratch=()):
    return pl.pallas_call(
        kernel,
        in_specs=specs,
        out_specs=out_specs or [BLOCK] * len(outs),
        scratch_shapes=scratch,
        out_shape=[jax.ShapeDtypeStruct(shape, dtype) for shape, dtype in outs],
        compiler_params=pltpu.CompilerParams(vmem_limit_bytes=24 * 2**20),
    )


def nn(left, right):
    return jnp.dot(left, right, preferred_element_type=jnp.float32)


def nt(left, right):
    return lax.dot_general(
        left, right, (((1,), (1,)), ((), ())), preferred_element_type=jnp.float32
    )


def tn(left, right):
    return lax.dot_general(
        left, right, (((0,), (0,)), ((), ())), preferred_element_type=jnp.float32
    )


def attend(
    flow_ref, mask_ref, noise_far, action_far, kv_far, sent_ref, resid_ref,
    noise_ref, action_ref, kv_ref, sems,
):
    copies = [
        pltpu.make_async_copy(far, near, sems.at[i])
        for i, (far, near) in enumerate(
            ((kv_far, kv_ref), (noise_far, noise_ref), (action_far, action_ref))
        )
    ]
    for copy in copies:
        copy.start()
    for copy in copies:
        copy.wait()
    acts, width = noise_ref.shape
    span = kv_ref.shape[3]
    heads = width // span
    time = (flow_ref[0].astype(jnp.float32) + 1.0) / (STEPS_T + 1.0)
    row = lax.broadcasted_iota(jnp.int32, (acts, 128), 0)
    mask = jnp.zeros((acts, 128), jnp.float32)
    for i in range(acts):
        mask = jnp.where(row == i, mask_ref[i].astype(jnp.float32), mask)
    mask = mask[:, :1]
    noisy = noise_ref[...].astype(jnp.float32)
    clean = action_ref[...].astype(jnp.float32)
    inputs = time * noisy + (1.0 - time) * clean
    queries = jnp.concatenate([inputs[:, i * span : (i + 1) * span] for i in range(heads)], 0)
    queries = queries * lax.rsqrt(jnp.mean(queries * queries, -1, keepdims=True) + epsilon)
    keys = kv_ref[0, 0].astype(jnp.float32)
    keys = keys * lax.rsqrt(jnp.mean(keys * keys, -1, keepdims=True) + epsilon)
    energies = nt(queries.astype(jnp.bfloat16), keys.astype(jnp.bfloat16))
    expo = jnp.exp(energies * (sharpness_divisor / span))
    weights = (expo / jnp.sum(expo, -1, keepdims=True)).astype(jnp.bfloat16)
    mixed = nn(weights, kv_ref[1, 0])
    mixed = jnp.concatenate([mixed[i * acts : (i + 1) * acts] for i in range(heads)], 1)
    hidden = inputs + mixed
    normed = hidden * lax.rsqrt(jnp.mean(hidden * hidden, -1, keepdims=True) + epsilon)
    normed = (normed.astype(jnp.bfloat16).astype(jnp.float32) * mask).astype(jnp.bfloat16)
    for i in range(sent_ref.shape[0]):
        sent_ref[i] = normed
    resid_ref[...] = mask * (hidden - (noisy - clean))


def forward(rows_ref, up_ref, query_ref, lin_ref, slopes_ref, curves_ref, tangent_ref):
    rows = rows_ref[...]
    pre = nn(rows, up_ref[...])
    sig = jax.nn.sigmoid(pre)
    slopes = sig * (1.0 + pre * (1.0 - sig))
    curves_ref[...] = sig * (1.0 - sig) * (2.0 + pre * (1.0 - 2.0 * sig))
    tangent = nn(rows, query_ref[...].astype(jnp.bfloat16))
    slopes_ref[...] = slopes
    tangent_ref[...] = tangent
    active = (pre * sig).astype(jnp.bfloat16)
    linear = (slopes * tangent).astype(jnp.bfloat16)
    lin_ref[:, :, 0] = active.reshape(4, 4, 16, -1)
    lin_ref[:, :, 1] = linear.reshape(4, 4, 16, -1)


def down(lin_ref, *refs):
    *blocks, out_ref = refs
    place = lax.axis_index("y")
    rows = out_ref.shape[0]
    out = 0.0
    for j, block in enumerate(blocks):
        source = lin_ref[lax.rem(place + j, 4)].reshape(rows, -1)
        out = out + nn(source, block[...])
    out_ref[...] = out.astype(jnp.bfloat16)


def pull(source_ref, *refs):
    *blocks, out_ref = refs
    place = lax.axis_index("y")
    if source_ref.ndim == 3:
        source = source_ref[0].astype(jnp.float32)
        for i in range(1, source_ref.shape[0]):
            source = source + source_ref[i].astype(jnp.float32)
        source = source.astype(jnp.bfloat16)
    else:
        source = source_ref[...]
    for j, block in enumerate(blocks):
        out_ref[lax.rem(place + j, 4)] = nt(source, block[...]).astype(jnp.bfloat16)


def halves(rows_ref, second, kept_ref, given_ref):
    half = D // 2
    low = tn(rows_ref[:, :half], second).astype(jnp.bfloat16)
    high = tn(rows_ref[:, half:], second).astype(jnp.bfloat16)
    core = lax.axis_index("c")

    @pl.when(core == 0)
    def _():
        kept_ref[...] = low
        given_ref[...] = high

    @pl.when(core == 1)
    def _():
        kept_ref[...] = high
        given_ref[...] = low


def curve_first(
    both_ref, slopes_ref, curves_ref, tangent_ref, rows_ref, kept_ref, given_ref, bend_ref, back_ref
):
    shape = slopes_ref.shape
    pulled = both_ref[:, :, 0].reshape(shape).astype(jnp.float32)
    moved = both_ref[:, :, 1].reshape(shape).astype(jnp.float32)
    slopes = slopes_ref[...]
    bend = pulled * curves_ref[...]
    bend_ref[...] = bend
    back_ref[...] = pulled * slopes
    second = (moved * slopes + bend * tangent_ref[...]).astype(jnp.bfloat16)
    halves(rows_ref, second, kept_ref, given_ref)


def turn(rows_ref, first_ref, slopes_ref, tangent_ref, lin_ref, along_ref):
    along = nn(rows_ref[...], first_ref[...]) / TOKENS
    along_ref[...] = along
    later = keep * tangent_ref[...] - along
    lin_ref[...] = (slopes_ref[...] * later).astype(jnp.bfloat16).reshape(lin_ref.shape)


def curve_second(
    moved_ref, slopes_ref, bend_ref, tangent_ref, along_ref, rows_ref, kept_ref, given_ref
):
    moved = moved_ref[...].reshape(slopes_ref.shape).astype(jnp.float32)
    later = keep * tangent_ref[...] - along_ref[...]
    second = (moved * slopes_ref[...] + bend_ref[...] * later).astype(jnp.bfloat16)
    halves(rows_ref, second, kept_ref, given_ref)


def score(
    rows_ref, second_ref, tangent_ref, along_ref, back_ref, first_ref, query_ref,
    terms_ref, vector_far, vector_ref, sem,
):
    first = first_ref[...].astype(jnp.float32)
    second = second_ref[...].astype(jnp.float32)
    vector_ref[...] = (1.0 + rest * keep) * query_ref[...] - (rest * first + second) / TOKENS
    copy = pltpu.make_async_copy(vector_ref, vector_far, sem)
    copy.start()
    along = nn(rows_ref[...], second_ref[...]) / TOKENS
    projected = (1.0 + rest * keep) * tangent_ref[...] - rest * along_ref[...] - along
    terms = (projected * back_ref[...]).reshape(16, 16, 256)
    terms = jnp.sum(terms[:, :, :128] + terms[:, :, 128:], 1, keepdims=True)
    terms_ref[...] = terms
    copy.wait()


def finish(terms_ref, score_ref):
    acts = TOKENS // 512
    score_ref[0] = -jnp.sum(terms_ref[...]) / (acts * math.sqrt(D * FF))


def join(kept_ref, both_ref, pair_ref):
    taken = both_ref[1 - lax.axis_index("c")].astype(jnp.float32)
    pair_ref[...] = (kept_ref[...].astype(jnp.float32) + taken).astype(jnp.bfloat16)


def swap(blocks, axes):
    return lax.all_to_all(blocks, axes, 0, 0)


def collect(block, axes, members):
    return swap(jnp.broadcast_to(block[None], (members, *block.shape)), axes)


def total(blocks):
    return jnp.sum(blocks.astype(jnp.float32), 0)


def sum_copies(kept, given):
    half, columns = kept.shape
    both = lax.all_gather(given, "c", axis=0)
    (pair,) = local(join, [BLOCK] * 2, [(kept.shape, kept.dtype)])(kept, both)
    rows = total(swap(pair.reshape(16, half // 16, columns), GRID))
    rows = collect(rows.astype(jnp.bfloat16), GRID, 16).reshape(half, columns)
    return lax.all_gather(rows, "c", axis=0, tiled=True)


def shards(noise_embed, action_embed, prefix_kv, flow_step, action_mask, w_up, w_down, query_grad):
    own = noise_embed.shape[0]
    tokens = own * 16
    units = w_up.shape[1]
    half = jnp.bfloat16
    full = jnp.float32
    square = ((tokens, units), full)
    blocks = [w_down]
    for shift in (1, 2, 3):
        blocks.append(lax.ppermute(w_down, "y", [((i + shift) % 4, i) for i in range(4)]))

    sent, resid = local(
        attend,
        [SCALARS, SCALARS, FAR, FAR, FAR],
        [((4, own, D), half), ((own, D), full)],
        scratch=[
            pltpu.VMEM(noise_embed.shape, half),
            pltpu.VMEM(action_embed.shape, half),
            pltpu.VMEM(prefix_kv.shape, half),
            pltpu.SemaphoreType.DMA((3,)),
        ],
    )(flow_step, action_mask, noise_embed, action_embed, prefix_kv)
    stage, blocks = lax.optimization_barrier((swap(sent, "zh"), blocks))
    rows = collect(stage, "y", 4).reshape(tokens, D)
    lin, slopes, curves, tangent = local(
        forward, [BLOCK] * 3, [((4, 4, 2, own, units), half), square, square, square]
    )(rows, w_up, query_grad)
    (stage,) = local(down, [BLOCK] * 5, [((8 * own, D), half)])(swap(lin, "y"), *blocks)
    both = total(swap(stage.reshape(4, 2, own, D), "zh"))
    both = jnp.stack([(resid + both[0]).astype(half), both[1].astype(half)])
    both = collect(both, "zh", 4).reshape(8 * own, D)
    (both,) = local(pull, [BLOCK] * 5, [((4, 8 * own, units), half)])(both, *blocks)
    both = swap(both, "y").reshape(4, 4, 2, own, units)
    sides = [((D // 2, units), half)] * 2
    kept, given, bend, back = local(curve_first, [BLOCK] * 5, [*sides, square, square])(
        both, slopes, curves, tangent, rows
    )
    first = sum_copies(kept, given)

    lin, along = local(turn, [BLOCK] * 4, [((4, 4 * own, units), half), square])(
        rows, first, slopes, tangent
    )
    (stage,) = local(down, [BLOCK] * 5, [((4 * own, D), half)])(swap(lin, "y"), *blocks)
    stage = lax.all_gather(stage, "zh", axis=0)
    (moved,) = local(pull, [BLOCK] * 5, [((4, 4 * own, units), half)])(stage, *blocks)
    kept, given = local(curve_second, [BLOCK] * 6, sides)(
        swap(moved, "y"), slopes, bend, tangent, along, rows
    )
    second = sum_copies(kept, given)

    terms, vector = local(
        score,
        [BLOCK] * 7,
        [((16, 1, 128), full), (query_grad.shape, full)],
        [BLOCK, FAR],
        [pltpu.VMEM(query_grad.shape, full), pltpu.SemaphoreType.DMA],
    )(rows, second, tangent, along, back, first, query_grad)
    (owned,) = local(finish, [BLOCK], [((1,), full)], [SCALARS])(swap(terms, ("y", "zh")))
    return (vector, owned)


def solution(mesh):
    fine = Mesh(mesh.devices.reshape(SIZES), AXES)
    fsdp, everyone = AXES[:2], AXES
    placed = (
        P(everyone, None),
        P(everyone, None),
        P(None, everyone, None, None),
        P(everyone),
        P(everyone),
        P(None, fsdp),
        P(fsdp, None),
        P(None, fsdp),
    )
    return jax.shard_map(
        shards,
        mesh=fine,
        in_specs=placed,
        out_specs=(P(None, fsdp), P(everyone)),
        check_vma=False,
    )
```

```python
import functools
import math

import jax
import jax.numpy as jnp
from jax import lax
from jax.experimental import pallas as pl
from jax.experimental.pallas import tpu as pltpu
from jax.sharding import Mesh
from jax.sharding import PartitionSpec as P

D = 1024
FF = 4096
STEPS_T = 10
TOKENS = 8192

epsilon = 1e-06
sharpness_divisor = 6.0
damping_factor = 0.01
rest = 1.0 - damping_factor
keep = 1.0 + rest

AXES = ("zh", "y", "x", "zl", "c")
SIZES = (4, 4, 4, 4, 2)
GRID = ("x", "zl")

SCALARS = pl.BlockSpec(memory_space=pltpu.SMEM)
BLOCK = pl.BlockSpec(memory_space=pltpu.VMEM)


FAR = pl.BlockSpec(memory_space=pltpu.HBM)


def local(kernel, specs, outs, out_specs=None, scratch=()):
    return pl.pallas_call(
        kernel,
        in_specs=specs,
        out_specs=out_specs or [BLOCK] * len(outs),
        scratch_shapes=scratch,
        out_shape=[jax.ShapeDtypeStruct(shape, dtype) for shape, dtype in outs],
        compiler_params=pltpu.CompilerParams(vmem_limit_bytes=24 * 2**20),
    )


def nn(left, right):
    return jnp.dot(left, right, preferred_element_type=jnp.float32)


def nt(left, right):
    return lax.dot_general(
        left, right, (((1,), (1,)), ((), ())), preferred_element_type=jnp.float32
    )


def tn(left, right):
    return lax.dot_general(
        left, right, (((0,), (0,)), ((), ())), preferred_element_type=jnp.float32
    )


def attend(
    flow_ref, mask_ref, noise_far, action_far, kv_far, sent_ref, resid_ref,
    noise_ref, action_ref, kv_ref, sems,
):
    copies = [
        pltpu.make_async_copy(far, near, sems.at[i])
        for i, (far, near) in enumerate(
            ((kv_far, kv_ref), (noise_far, noise_ref), (action_far, action_ref))
        )
    ]
    for copy in copies:
        copy.start()
    for copy in copies:
        copy.wait()
    acts, width = noise_ref.shape
    span = kv_ref.shape[3]
    heads = width // span
    time = (flow_ref[0].astype(jnp.float32) + 1.0) / (STEPS_T + 1.0)
    row = lax.broadcasted_iota(jnp.int32, (acts, 128), 0)
    mask = jnp.zeros((acts, 128), jnp.float32)
    for i in range(acts):
        mask = jnp.where(row == i, mask_ref[i].astype(jnp.float32), mask)
    mask = mask[:, :1]
    noisy = noise_ref[...].astype(jnp.float32)
    clean = action_ref[...].astype(jnp.float32)
    inputs = time * noisy + (1.0 - time) * clean
    queries = jnp.concatenate([inputs[:, i * span : (i + 1) * span] for i in range(heads)], 0)
    queries = queries * lax.rsqrt(jnp.mean(queries * queries, -1, keepdims=True) + epsilon)
    keys = kv_ref[0, 0].astype(jnp.float32)
    keys = keys * lax.rsqrt(jnp.mean(keys * keys, -1, keepdims=True) + epsilon)
    energies = nt(queries.astype(jnp.bfloat16), keys.astype(jnp.bfloat16))
    expo = jnp.exp(energies * (sharpness_divisor / span))
    weights = (expo / jnp.sum(expo, -1, keepdims=True)).astype(jnp.bfloat16)
    mixed = nn(weights, kv_ref[1, 0])
    mixed = jnp.concatenate([mixed[i * acts : (i + 1) * acts] for i in range(heads)], 1)
    hidden = inputs + mixed
    normed = hidden * lax.rsqrt(jnp.mean(hidden * hidden, -1, keepdims=True) + epsilon)
    normed = (normed.astype(jnp.bfloat16).astype(jnp.float32) * mask).astype(jnp.bfloat16)
    for i in range(sent_ref.shape[0]):
        sent_ref[i] = normed
    resid_ref[...] = mask * (hidden - (noisy - clean))


def forward(rows_ref, up_ref, query_ref, lin_ref, slopes_ref, curves_ref, tangent_ref):
    rows = rows_ref[...]
    pre = nn(rows, up_ref[...])
    sig = jax.nn.sigmoid(pre)
    slopes = sig * (1.0 + pre * (1.0 - sig))
    curves_ref[...] = sig * (1.0 - sig) * (2.0 + pre * (1.0 - 2.0 * sig))
    tangent = nn(rows, query_ref[...].astype(jnp.bfloat16))
    slopes_ref[...] = slopes
    tangent_ref[...] = tangent
    active = (pre * sig).astype(jnp.bfloat16)
    linear = (slopes * tangent).astype(jnp.bfloat16)
    lin_ref[:, :, 0] = active.reshape(4, 4, 16, -1)
    lin_ref[:, :, 1] = linear.reshape(4, 4, 16, -1)


def down(lin_ref, *refs):
    *blocks, out_ref = refs
    place = lax.axis_index("y")
    rows = out_ref.shape[0]
    out = 0.0
    for j, block in enumerate(blocks):
        source = lin_ref[lax.rem(place + j, 4)].reshape(rows, -1)
        out = out + nn(source, block[...])
    out_ref[...] = out.astype(jnp.bfloat16)


def pull(source_ref, *refs):
    *blocks, out_ref = refs
    place = lax.axis_index("y")
    if source_ref.ndim == 3:
        source = source_ref[0].astype(jnp.float32)
        for i in range(1, source_ref.shape[0]):
            source = source + source_ref[i].astype(jnp.float32)
        source = source.astype(jnp.bfloat16)
    else:
        source = source_ref[...]
    for j, block in enumerate(blocks):
        out_ref[lax.rem(place + j, 4)] = nt(source, block[...]).astype(jnp.bfloat16)


def halves(rows_ref, second, kept_ref, given_ref):
    half = D // 2
    low = tn(rows_ref[:, :half], second).astype(jnp.bfloat16)
    high = tn(rows_ref[:, half:], second).astype(jnp.bfloat16)
    core = lax.axis_index("c")

    @pl.when(core == 0)
    def _():
        kept_ref[...] = low
        given_ref[...] = high

    @pl.when(core == 1)
    def _():
        kept_ref[...] = high
        given_ref[...] = low


def curve_first(
    both_ref, slopes_ref, curves_ref, tangent_ref, rows_ref, kept_ref, given_ref, bend_ref, back_ref
):
    shape = slopes_ref.shape
    pulled = both_ref[:, :, 0].reshape(shape).astype(jnp.float32)
    moved = both_ref[:, :, 1].reshape(shape).astype(jnp.float32)
    slopes = slopes_ref[...]
    bend = pulled * curves_ref[...]
    bend_ref[...] = bend
    back_ref[...] = pulled * slopes
    second = (moved * slopes + bend * tangent_ref[...]).astype(jnp.bfloat16)
    halves(rows_ref, second, kept_ref, given_ref)


def turn(rows_ref, first_ref, slopes_ref, tangent_ref, lin_ref, along_ref):
    along = nn(rows_ref[...], first_ref[...]) / TOKENS
    along_ref[...] = along
    later = keep * tangent_ref[...] - along
    lin_ref[...] = (slopes_ref[...] * later).astype(jnp.bfloat16).reshape(lin_ref.shape)


def curve_second(
    moved_ref, slopes_ref, bend_ref, tangent_ref, along_ref, rows_ref, kept_ref, given_ref
):
    moved = moved_ref[...].reshape(slopes_ref.shape).astype(jnp.float32)
    later = keep * tangent_ref[...] - along_ref[...]
    second = (moved * slopes_ref[...] + bend_ref[...] * later).astype(jnp.bfloat16)
    halves(rows_ref, second, kept_ref, given_ref)


def score(
    rows_ref, second_ref, tangent_ref, along_ref, back_ref, first_ref, query_ref,
    terms_ref, vector_far, vector_ref, sem,
):
    first = first_ref[...].astype(jnp.float32)
    second = second_ref[...].astype(jnp.float32)
    vector_ref[...] = (1.0 + rest * keep) * query_ref[...] - (rest * first + second) / TOKENS
    copy = pltpu.make_async_copy(vector_ref, vector_far, sem)
    copy.start()
    along = nn(rows_ref[...], second_ref[...]) / TOKENS
    projected = (1.0 + rest * keep) * tangent_ref[...] - rest * along_ref[...] - along
    terms = (projected * back_ref[...]).reshape(16, 16, 256)
    terms = jnp.sum(terms[:, :, :128] + terms[:, :, 128:], 1, keepdims=True)
    terms_ref[...] = terms
    copy.wait()


def finish(terms_ref, score_ref):
    acts = TOKENS // 512
    score_ref[0] = -jnp.sum(terms_ref[...]) / (acts * math.sqrt(D * FF))


def join(kept_ref, both_ref, pair_ref):
    taken = both_ref[1 - lax.axis_index("c")].astype(jnp.float32)
    pair_ref[...] = (kept_ref[...].astype(jnp.float32) + taken).astype(jnp.bfloat16)


def spread(blocks_ref, copies_ref):
    out = blocks_ref[0].astype(jnp.float32)
    for i in range(1, blocks_ref.shape[0]):
        out = out + blocks_ref[i].astype(jnp.float32)
    out = out.astype(jnp.bfloat16)
    for i in range(copies_ref.shape[0]):
        copies_ref[i] = out


def swap(blocks, axes):
    return lax.all_to_all(blocks, axes, 0, 0)


def collect(block, axes, members):
    return swap(jnp.broadcast_to(block[None], (members, *block.shape)), axes)


def total(blocks):
    return jnp.sum(blocks.astype(jnp.float32), 0)


def sum_copies(kept, given):
    half, columns = kept.shape
    both = lax.all_gather(given, "c", axis=0)
    (pair,) = local(join, [BLOCK] * 2, [(kept.shape, kept.dtype)])(kept, both)
    shape = (16, half // 16, columns)
    (rows,) = local(spread, [BLOCK], [(shape, pair.dtype)])(swap(pair.reshape(shape), GRID))
    rows = swap(rows, GRID).reshape(half, columns)
    return lax.all_gather(rows, "c", axis=0, tiled=True)


def shards(noise_embed, action_embed, prefix_kv, flow_step, action_mask, w_up, w_down, query_grad):
    own = noise_embed.shape[0]
    tokens = own * 16
    units = w_up.shape[1]
    half = jnp.bfloat16
    full = jnp.float32
    square = ((tokens, units), full)
    blocks = [w_down]
    for shift in (1, 2, 3):
        blocks.append(lax.ppermute(w_down, "y", [((i + shift) % 4, i) for i in range(4)]))

    sent, resid = local(
        attend,
        [SCALARS, SCALARS, FAR, FAR, FAR],
        [((4, own, D), half), ((own, D), full)],
        scratch=[
            pltpu.VMEM(noise_embed.shape, half),
            pltpu.VMEM(action_embed.shape, half),
            pltpu.VMEM(prefix_kv.shape, half),
            pltpu.SemaphoreType.DMA((3,)),
        ],
    )(flow_step, action_mask, noise_embed, action_embed, prefix_kv)
    stage, blocks = lax.optimization_barrier((swap(sent, "zh"), blocks))
    rows = collect(stage, "y", 4).reshape(tokens, D)
    lin, slopes, curves, tangent = local(
        forward, [BLOCK] * 3, [((4, 4, 2, own, units), half), square, square, square]
    )(rows, w_up, query_grad)
    (stage,) = local(down, [BLOCK] * 5, [((8 * own, D), half)])(swap(lin, "y"), *blocks)
    both = total(swap(stage.reshape(4, 2, own, D), "zh"))
    both = jnp.stack([(resid + both[0]).astype(half), both[1].astype(half)])
    both = collect(both, "zh", 4).reshape(8 * own, D)
    (both,) = local(pull, [BLOCK] * 5, [((4, 8 * own, units), half)])(both, *blocks)
    both = swap(both, "y").reshape(4, 4, 2, own, units)
    sides = [((D // 2, units), half)] * 2
    kept, given, bend, back = local(curve_first, [BLOCK] * 5, [*sides, square, square])(
        both, slopes, curves, tangent, rows
    )
    first = sum_copies(kept, given)

    lin, along = local(turn, [BLOCK] * 4, [((4, 4 * own, units), half), square])(
        rows, first, slopes, tangent
    )
    (stage,) = local(down, [BLOCK] * 5, [((4 * own, D), half)])(swap(lin, "y"), *blocks)
    stage = lax.all_gather(stage, "zh", axis=0)
    (moved,) = local(pull, [BLOCK] * 5, [((4, 4 * own, units), half)])(stage, *blocks)
    kept, given = local(curve_second, [BLOCK] * 6, sides)(
        swap(moved, "y"), slopes, bend, tangent, along, rows
    )
    second = sum_copies(kept, given)

    terms, vector = local(
        score,
        [BLOCK] * 7,
        [((16, 1, 128), full), (query_grad.shape, full)],
        [BLOCK, FAR],
        [pltpu.VMEM(query_grad.shape, full), pltpu.SemaphoreType.DMA],
    )(rows, second, tangent, along, back, first, query_grad)
    (owned,) = local(finish, [BLOCK], [((1,), full)], [SCALARS])(swap(terms, ("y", "zh")))
    return (vector, owned)


def solution(mesh):
    fine = Mesh(mesh.devices.reshape(SIZES), AXES)
    fsdp, everyone = AXES[:2], AXES
    placed = (
        P(everyone, None),
        P(everyone, None),
        P(None, everyone, None, None),
        P(everyone),
        P(everyone),
        P(None, fsdp),
        P(fsdp, None),
        P(None, fsdp),
    )
    return jax.shard_map(
        shards,
        mesh=fine,
        in_specs=placed,
        out_specs=(P(None, fsdp), P(everyone)),
        check_vma=False,
    )
```

```python
import functools
import math

import jax
import jax.numpy as jnp
from jax import lax
from jax.experimental import pallas as pl
from jax.experimental.pallas import tpu as pltpu
from jax.sharding import Mesh
from jax.sharding import PartitionSpec as P

D = 1024
FF = 4096
STEPS_T = 10
TOKENS = 8192

epsilon = 1e-06
sharpness_divisor = 6.0
damping_factor = 0.01
rest = 1.0 - damping_factor
keep = 1.0 + rest

AXES = ("zh", "y", "x", "zl", "c")
SIZES = (4, 4, 4, 4, 2)
GRID = ("x", "zl")

SCALARS = pl.BlockSpec(memory_space=pltpu.SMEM)
BLOCK = pl.BlockSpec(memory_space=pltpu.VMEM)


FAR = pl.BlockSpec(memory_space=pltpu.HBM)


def local(kernel, specs, outs, out_specs=None, scratch=()):
    return pl.pallas_call(
        kernel,
        in_specs=specs,
        out_specs=out_specs or [BLOCK] * len(outs),
        scratch_shapes=scratch,
        out_shape=[jax.ShapeDtypeStruct(shape, dtype) for shape, dtype in outs],
        compiler_params=pltpu.CompilerParams(vmem_limit_bytes=24 * 2**20),
    )


def nn(left, right):
    return jnp.dot(left, right, preferred_element_type=jnp.float32)


def nt(left, right):
    return lax.dot_general(
        left, right, (((1,), (1,)), ((), ())), preferred_element_type=jnp.float32
    )


def tn(left, right):
    return lax.dot_general(
        left, right, (((0,), (0,)), ((), ())), preferred_element_type=jnp.float32
    )


def attend(
    flow_ref, mask_ref, noise_far, action_far, kv_far, sent_ref, resid_ref,
    noise_ref, action_ref, kv_ref, sems,
):
    copies = [
        pltpu.make_async_copy(far, near, sems.at[i])
        for i, (far, near) in enumerate(
            ((kv_far, kv_ref), (noise_far, noise_ref), (action_far, action_ref))
        )
    ]
    for copy in copies:
        copy.start()
    for copy in copies:
        copy.wait()
    acts, width = noise_ref.shape
    span = kv_ref.shape[3]
    heads = width // span
    time = (flow_ref[0].astype(jnp.float32) + 1.0) / (STEPS_T + 1.0)
    row = lax.broadcasted_iota(jnp.int32, (acts, 128), 0)
    mask = jnp.zeros((acts, 128), jnp.float32)
    for i in range(acts):
        mask = jnp.where(row == i, mask_ref[i].astype(jnp.float32), mask)
    mask = mask[:, :1]
    noisy = noise_ref[...].astype(jnp.float32)
    clean = action_ref[...].astype(jnp.float32)
    inputs = time * noisy + (1.0 - time) * clean
    queries = jnp.concatenate([inputs[:, i * span : (i + 1) * span] for i in range(heads)], 0)
    queries = queries * lax.rsqrt(jnp.mean(queries * queries, -1, keepdims=True) + epsilon)
    keys = kv_ref[0, 0].astype(jnp.float32)
    keys = keys * lax.rsqrt(jnp.mean(keys * keys, -1, keepdims=True) + epsilon)
    energies = nt(queries.astype(jnp.bfloat16), keys.astype(jnp.bfloat16))
    expo = jnp.exp(energies * (sharpness_divisor / span))
    weights = (expo / jnp.sum(expo, -1, keepdims=True)).astype(jnp.bfloat16)
    mixed = nn(weights, kv_ref[1, 0])
    mixed = jnp.concatenate([mixed[i * acts : (i + 1) * acts] for i in range(heads)], 1)
    hidden = inputs + mixed
    normed = hidden * lax.rsqrt(jnp.mean(hidden * hidden, -1, keepdims=True) + epsilon)
    normed = (normed.astype(jnp.bfloat16).astype(jnp.float32) * mask).astype(jnp.bfloat16)
    for i in range(sent_ref.shape[0]):
        sent_ref[i] = normed
    resid_ref[...] = mask * (hidden - (noisy - clean))


def forward(rows_ref, up_ref, query_ref, lin_ref, slopes_ref, curves_ref, tangent_ref):
    rows = rows_ref[...]
    pre = nn(rows, up_ref[...])
    sig = jax.nn.sigmoid(pre)
    slopes = sig * (1.0 + pre * (1.0 - sig))
    curves_ref[...] = sig * (1.0 - sig) * (2.0 + pre * (1.0 - 2.0 * sig))
    tangent = nn(rows, query_ref[...].astype(jnp.bfloat16))
    slopes_ref[...] = slopes
    tangent_ref[...] = tangent
    active = (pre * sig).astype(jnp.bfloat16)
    linear = (slopes * tangent).astype(jnp.bfloat16)
    lin_ref[:, :, 0] = active.reshape(4, 4, 16, -1)
    lin_ref[:, :, 1] = linear.reshape(4, 4, 16, -1)


def down(lin_ref, *refs):
    *blocks, out_ref = refs
    place = lax.axis_index("y")
    rows = out_ref.shape[0]
    out = 0.0
    for j, block in enumerate(blocks):
        source = lin_ref[lax.rem(place + j, 4)].reshape(rows, -1)
        out = out + nn(source, block[...])
    out_ref[...] = out.astype(jnp.bfloat16)


def pull(source_ref, *refs):
    *blocks, out_ref = refs
    place = lax.axis_index("y")
    if source_ref.ndim == 3:
        source = source_ref[0].astype(jnp.float32)
        for i in range(1, source_ref.shape[0]):
            source = source + source_ref[i].astype(jnp.float32)
        source = source.astype(jnp.bfloat16)
    else:
        source = source_ref[...]
    for j, block in enumerate(blocks):
        out_ref[lax.rem(place + j, 4)] = nt(source, block[...]).astype(jnp.bfloat16)


def halves(rows_ref, second, kept_ref, given_ref):
    half = D // 2
    low = tn(rows_ref[:, :half], second).astype(jnp.bfloat16)
    high = tn(rows_ref[:, half:], second).astype(jnp.bfloat16)
    core = lax.axis_index("c")

    @pl.when(core == 0)
    def _():
        kept_ref[...] = low
        given_ref[...] = high

    @pl.when(core == 1)
    def _():
        kept_ref[...] = high
        given_ref[...] = low


def curve_first(
    both_ref, slopes_ref, curves_ref, tangent_ref, rows_ref, kept_ref, given_ref, bend_ref, back_ref
):
    shape = slopes_ref.shape
    pulled = both_ref[:, :, 0].reshape(shape).astype(jnp.float32)
    moved = both_ref[:, :, 1].reshape(shape).astype(jnp.float32)
    slopes = slopes_ref[...]
    bend = pulled * curves_ref[...]
    bend_ref[...] = bend
    back_ref[...] = pulled * slopes
    second = (moved * slopes + bend * tangent_ref[...]).astype(jnp.bfloat16)
    halves(rows_ref, second, kept_ref, given_ref)


def turn(rows_ref, first_ref, slopes_ref, tangent_ref, lin_ref, along_ref):
    along = nn(rows_ref[...], first_ref[...]) / TOKENS
    along_ref[...] = along
    later = keep * tangent_ref[...] - along
    lin_ref[...] = (slopes_ref[...] * later).astype(jnp.bfloat16).reshape(lin_ref.shape)


def curve_second(
    moved_ref, slopes_ref, bend_ref, tangent_ref, along_ref, rows_ref, kept_ref, given_ref
):
    moved = moved_ref[...].reshape(slopes_ref.shape).astype(jnp.float32)
    later = keep * tangent_ref[...] - along_ref[...]
    second = (moved * slopes_ref[...] + bend_ref[...] * later).astype(jnp.bfloat16)
    halves(rows_ref, second, kept_ref, given_ref)


def score(
    rows_ref, second_ref, tangent_ref, along_ref, back_ref, first_ref, query_ref,
    terms_ref, vector_far, vector_ref, sem,
):
    first = first_ref[...].astype(jnp.float32)
    second = second_ref[...].astype(jnp.float32)
    vector_ref[...] = (1.0 + rest * keep) * query_ref[...] - (rest * first + second) / TOKENS
    copy = pltpu.make_async_copy(vector_ref, vector_far, sem)
    copy.start()
    along = nn(rows_ref[...], second_ref[...]) / TOKENS
    projected = (1.0 + rest * keep) * tangent_ref[...] - rest * along_ref[...] - along
    terms = (projected * back_ref[...]).reshape(16, 16, 256)
    terms = jnp.sum(terms[:, :, :128] + terms[:, :, 128:], 1, keepdims=True)
    terms_ref[...] = terms
    copy.wait()


def finish(terms_ref, score_ref):
    acts = TOKENS // 512
    score_ref[0] = -jnp.sum(terms_ref[...]) / (acts * math.sqrt(D * FF))


def join(kept_ref, both_ref, pair_ref):
    taken = both_ref[1 - lax.axis_index("c")].astype(jnp.float32)
    pair_ref[...] = (kept_ref[...].astype(jnp.float32) + taken).astype(jnp.bfloat16)


def spread(blocks_ref, copies_ref):
    out = blocks_ref[0].astype(jnp.float32)
    for i in range(1, blocks_ref.shape[0]):
        out = out + blocks_ref[i].astype(jnp.float32)
    out = out.astype(jnp.bfloat16)
    for i in range(copies_ref.shape[0]):
        copies_ref[i] = out


def settle(blocks_ref, resid_ref, copies_ref):
    out = blocks_ref[0].astype(jnp.float32)
    for i in range(1, blocks_ref.shape[0]):
        out = out + blocks_ref[i].astype(jnp.float32)
    err = (resid_ref[...] + out[0]).astype(jnp.bfloat16)
    moved = out[1].astype(jnp.bfloat16)
    for i in range(copies_ref.shape[0]):
        copies_ref[i, 0] = err
        copies_ref[i, 1] = moved


def swap(blocks, axes):
    return lax.all_to_all(blocks, axes, 0, 0)


def collect(block, axes, members):
    return swap(jnp.broadcast_to(block[None], (members, *block.shape)), axes)


def sum_copies(kept, given):
    half, columns = kept.shape
    both = lax.all_gather(given, "c", axis=0)
    (pair,) = local(join, [BLOCK] * 2, [(kept.shape, kept.dtype)])(kept, both)
    shape = (16, half // 16, columns)
    (rows,) = local(spread, [BLOCK], [(shape, pair.dtype)])(swap(pair.reshape(shape), GRID))
    rows = swap(rows, GRID).reshape(half, columns)
    return lax.all_gather(rows, "c", axis=0, tiled=True)


def shards(noise_embed, action_embed, prefix_kv, flow_step, action_mask, w_up, w_down, query_grad):
    own = noise_embed.shape[0]
    tokens = own * 16
    units = w_up.shape[1]
    half = jnp.bfloat16
    full = jnp.float32
    square = ((tokens, units), full)
    blocks = [w_down]
    for shift in (1, 2, 3):
        blocks.append(lax.ppermute(w_down, "y", [((i + shift) % 4, i) for i in range(4)]))

    sent, resid = local(
        attend,
        [SCALARS, SCALARS, FAR, FAR, FAR],
        [((4, own, D), half), ((own, D), full)],
        scratch=[
            pltpu.VMEM(noise_embed.shape, half),
            pltpu.VMEM(action_embed.shape, half),
            pltpu.VMEM(prefix_kv.shape, half),
            pltpu.SemaphoreType.DMA((3,)),
        ],
    )(flow_step, action_mask, noise_embed, action_embed, prefix_kv)
    stage, blocks = lax.optimization_barrier((swap(sent, "zh"), blocks))
    rows = collect(stage, "y", 4).reshape(tokens, D)
    lin, slopes, curves, tangent = local(
        forward, [BLOCK] * 3, [((4, 4, 2, own, units), half), square, square, square]
    )(rows, w_up, query_grad)
    (stage,) = local(down, [BLOCK] * 5, [((8 * own, D), half)])(swap(lin, "y"), *blocks)
    both = swap(stage.reshape(4, 2, own, D), "zh")
    (both,) = local(settle, [BLOCK] * 2, [(both.shape, half)])(both, resid)
    both = swap(both, "zh").reshape(8 * own, D)
    (both,) = local(pull, [BLOCK] * 5, [((4, 8 * own, units), half)])(both, *blocks)
    both = swap(both, "y").reshape(4, 4, 2, own, units)
    sides = [((D // 2, units), half)] * 2
    kept, given, bend, back = local(curve_first, [BLOCK] * 5, [*sides, square, square])(
        both, slopes, curves, tangent, rows
    )
    first = sum_copies(kept, given)

    lin, along = local(turn, [BLOCK] * 4, [((4, 4 * own, units), half), square])(
        rows, first, slopes, tangent
    )
    (stage,) = local(down, [BLOCK] * 5, [((4 * own, D), half)])(swap(lin, "y"), *blocks)
    stage = lax.all_gather(stage, "zh", axis=0)
    (moved,) = local(pull, [BLOCK] * 5, [((4, 4 * own, units), half)])(stage, *blocks)
    kept, given = local(curve_second, [BLOCK] * 6, sides)(
        swap(moved, "y"), slopes, bend, tangent, along, rows
    )
    second = sum_copies(kept, given)

    terms, vector = local(
        score,
        [BLOCK] * 7,
        [((16, 1, 128), full), (query_grad.shape, full)],
        [BLOCK, FAR],
        [pltpu.VMEM(query_grad.shape, full), pltpu.SemaphoreType.DMA],
    )(rows, second, tangent, along, back, first, query_grad)
    (owned,) = local(finish, [BLOCK], [((1,), full)], [SCALARS])(swap(terms, ("y", "zh")))
    return (vector, owned)


def solution(mesh):
    fine = Mesh(mesh.devices.reshape(SIZES), AXES)
    fsdp, everyone = AXES[:2], AXES
    placed = (
        P(everyone, None),
        P(everyone, None),
        P(None, everyone, None, None),
        P(everyone),
        P(everyone),
        P(None, fsdp),
        P(fsdp, None),
        P(None, fsdp),
    )
    return jax.shard_map(
        shards,
        mesh=fine,
        in_specs=placed,
        out_specs=(P(None, fsdp), P(everyone)),
        check_vma=False,
    )
```
